256 devices in a mesh: pre: 8 (over z), dec: 16 (over y, x), rep: 2 (over core).
Axes of the slice: x: 4, y: 4, z: 8, core: 2. Of those that a mesh axis runs over, the one named last changes fastest.
Arguments:
- queries: bfloat16 [96, 256, 8192], P(('rep', 'pre'), None, 'dec'), parts along dimension 0, may hold values from -0.59765625 to 0.59765625
- keys: bfloat16 [96, 256, 8192], P(('rep', 'pre'), None, 'dec'), parts along dimension 0, may hold values from -1.5 to 1.5
- values: bfloat16 [96, 256, 8192], P(('rep', 'pre'), None, 'dec'), parts along dimension 0, may hold values from -6 to 6
- log_decay: float32 [96, 256, 64], P(('rep', 'pre'), None, 'dec'), parts along dimension 0, may hold values from -2 to 0
- prior_state: float32 [96, 64, 128, 128], P(('rep', 'pre'), 'dec'), parts along dimension 0, may hold values from -6 to 6
- lengths: int32 [96], P(('rep', 'pre')), parts along dimension 0, may hold values from 1 to 256, 6272 in all
- owners: int32 [96, 1], P(('rep', 'pre')), parts along dimension 0, may hold values from 0 to 15; in each aligned block of 6 rows (0 to 5, 6 to 11, ...) no two rows name the same one
Outputs:
- prefill_out: bfloat16 [96, 256, 8192], P(('rep', 'pre'), None, 'dec'), parts along dimension 0
- decode_state: float32 [256, 64, 128, 128], P(('rep', 'dec'), 'pre'), parts along dimension 0
The draws below stay inside these ranges and needn't reach their ends.
There are 2 independent parts, one for each index of `rep`. The reference program is written for one: setup_inputs(seed, part) draws one part's arguments, and reference() takes and returns one part's arrays. A program takes and returns all parts, laid end to end along the dimension named above; each array names one. Nothing has to cross between parts.
Inputs may be any that keep to these rules, and one draw needn't show every extreme that they name: `owners`: in each aligned block of 6 rows no owner stands more than 1 times, and some owner exactly so often; every owner stands somewhere. The lengths sum to 48 * 256 // 2 + 256 // 2; the longest is 256.
All inputs are finite; a program needn't handle non-finite values. No bound on the sum of `lengths` on one device may be relied on, other than what follows from the above.
Results may differ from the reference program's by a relative error of at most 0.0047.
Values sent between devices are 32-bit elements; how exact they have to be, the bound alone decides.
No kernel may reach another device: no remote copies, remote signals or barrier semaphores. Data moves between devices by JAX's collectives and lax.ppermute only.
A program may use at most 128 MiB of HBM per device.

```python
import math
import jax
import jax.numpy as jnp
import numpy as np
from jax import lax

ATTENDER_NUMBER = 64
HD = 128
REQ_DEV = 6
CLOSING_TOKENS = 256
PAIR = 1
QUERY_SEQUENCES = 48
N_PRE = 8
N_DEC = 16


def draw_log_decay(key, part):
    key = jax.random.fold_in(key, 11)
    first, second, third, quarter_section, fifth = jax.random.split(key, 5)
    slow = math.log(2.3 / CLOSING_TOKENS)
    fast = math.log(1.0 / 40.0)
    mixing = jax.random.uniform(first, (1, 1, ATTENDER_NUMBER), jnp.float32)
    starting_memory = jnp.exp(slow + mixing * (fast - slow))
    attenuation_ratio = jnp.exp(jax.random.uniform(second, (QUERY_SEQUENCES, 1, 1), jnp.float32, minval=-0.35, maxval=0.35))
    unmasked_logits = jax.random.uniform(third, (QUERY_SEQUENCES, CLOSING_TOKENS, ATTENDER_NUMBER), jnp.float32, minval=0.5, maxval=1.5)
    current_segment = jax.random.uniform(quarter_section, (QUERY_SEQUENCES, CLOSING_TOKENS, ATTENDER_NUMBER), jnp.float32) < 3.0 / CLOSING_TOKENS
    falloff_multiplier = jnp.log(jax.random.uniform(fifth, (QUERY_SEQUENCES, CLOSING_TOKENS, ATTENDER_NUMBER), jnp.float32, minval=0.5, maxval=0.8))
    return (-(starting_memory * attenuation_ratio * unmasked_logits) + jnp.where(current_segment, falloff_multiplier, 0.0)).astype(jnp.float32)


def steps_of(own_key, dims, cuts, smallest, largest):
    loudness = 1.0
    for axis_at, blocks in cuts:
        heights = jax.random.uniform(jax.random.fold_in(jax.random.fold_in(own_key, 6), axis_at), (blocks,), jnp.float32, smallest / len(cuts), largest / len(cuts))
        loudness = loudness * jnp.repeat(jnp.exp(heights), dims[axis_at] // blocks).reshape((-1,) + (1,) * (len(dims) - 1 - axis_at))
    return loudness


def split_up(count, total, reach, slope):
    weights = [(1 << 20) // math.isqrt(grade ** slope) + 1 for grade in range(2, count + 1)]
    surplus, counts = total - reach - (count - 1), [1] * (count - 1)
    while surplus > 0:
        free = [i for i in range(count - 1) if counts[i] < reach]
        whole, budget = sum([weights[i] for i in free]), surplus
        for i in free:
            more = min(reach - counts[i], max(1, budget * weights[i] // whole), surplus)
            counts[i] = counts[i] + more
            surplus = surplus - more
    return np.array([reach] + counts)


def uneven_parts(key, number_of, total, most, slope):
    if number_of == 2:
        one = jax.random.randint(key, (), max(1, total - most), min(most, total - 1) + 1)
        return jnp.stack([one, total - one])
    sizes = jnp.asarray(split_up(number_of, total, most, slope), jnp.int32)
    twos = (number_of - 1) // 2
    donor, sink = sizes[1:1 + 2 * twos:2], sizes[2:2 + 2 * twos:2]
    margin = jnp.minimum(donor - 1, most - sink)
    passed = jax.random.randint(jax.random.fold_in(key, 1), (twos,), 0, 1 << 20) % (margin + 1)
    sizes = sizes.at[1:1 + 2 * twos:2].set(donor - passed).at[2:2 + 2 * twos:2].set(sink + passed)
    return sizes[jax.random.permutation(jax.random.fold_in(key, 2), number_of)]


def routed_block(key, own, number, rows, count, top, bound, lean):
    sequence = jax.random.permutation(key, count)
    crowded, common = portions_of(count, rows * top, bound, lean, True), portions_of(count, rows * top, bound, lean, False)
    places = jnp.arange(count)

    def named(sizes, offset_by):
        used = int((sizes > 0).sum())
        fixed = max(1, used // 4)
        shifted = fixed + (places - fixed + offset_by * (used - fixed)) % max(1, count - fixed)
        return jnp.zeros((count,), jnp.int32).at[sequence[jnp.where(places < fixed, places, shifted)]].set(jnp.asarray(sizes, jnp.int32))

    sizes = jnp.where(number % 4 == 0, named(crowded, number // 4), named(common, number - number // 4 - 1))
    mixed = jax.random.permutation(jax.random.fold_in(own, 3), count)
    source_of, taker = mixed[0:count // 2 * 2:2], mixed[1:count // 2 * 2:2]
    room = jnp.minimum(sizes[source_of] - 1, bound - sizes[taker]) // 2
    room = jnp.where((source_of == sequence[0]) | (taker == sequence[0]) | (sizes[taker] == 0), 0, jnp.maximum(room, 0))
    shifted = jax.random.randint(jax.random.fold_in(own, 4), (count // 2,), 0, 1 << 20) % (room + 1)
    sizes = sizes.at[source_of].add(-shifted).at[taker].add(shifted)
    items = jnp.searchsorted(jnp.cumsum(sizes), jnp.arange(rows * top), side="right").astype(jnp.int32)
    listing = items.reshape(top, rows).T
    listing = listing[jax.random.permutation(jax.random.fold_in(own, 1), rows)]
    offset_by = jax.random.randint(jax.random.fold_in(own, 2), (rows, 1), 0, top)
    return jnp.take_along_axis(listing, (jnp.arange(top)[None, :] + offset_by) % top, axis=1)


def portions_of(amount, total, reach, slope, full):
    loads = [(1 << 20) // math.isqrt(grade ** slope) + 1 for grade in range(1, amount + 1)]
    largest = reach if full else min(reach, max(-(-total // amount), total * loads[0] // sum(loads)))
    least = 1 if total - largest >= amount - 1 else 0
    holding, rest = [largest] + [least] * (amount - 1), total - largest - least * (amount - 1)
    while rest > 0:
        free = [i for i in range(1, amount) if holding[i] < largest] or [i for i in range(1, amount) if holding[i] < reach]
        pool, left = sum([loads[i] for i in free]), rest
        for i in free:
            more = min(reach - holding[i], max(1, left * loads[i] // pool), rest)
            holding[i] = holding[i] + more
            rest = rest - more
    return np.array(holding)


def bell_draw(key, shape, scale, reach, pieces=(), kind=jnp.bfloat16):
    gain = steps_of(key, shape, pieces, -0.22, 0.18) if pieces else 1.0
    array = jax.random.normal(key, shape, jnp.float32) * scale * gain
    return jnp.minimum(jnp.maximum(array, -reach), reach).astype(kind)


def setup_inputs(seed: int = 0, part: int = 0) -> dict:
    key_of = jax.random.split(jax.random.key(seed), 8)
    part_splits = jax.random.split(jax.random.fold_in(key_of[7], part), 8)
    queries = bell_draw(part_splits[0], (QUERY_SEQUENCES, CLOSING_TOKENS, ATTENDER_NUMBER * HD), 0.088, 0.59765625, ((0, 8), (2, 16)))
    keys = bell_draw(part_splits[1], (QUERY_SEQUENCES, CLOSING_TOKENS, ATTENDER_NUMBER * HD), 0.25, 1.5, ((0, 8), (2, 16)))
    values = bell_draw(part_splits[2], (QUERY_SEQUENCES, CLOSING_TOKENS, ATTENDER_NUMBER * HD), 1.0, 6.0, ((0, 8), (2, 16)))
    log_decay = draw_log_decay(jax.random.fold_in(jax.random.fold_in(key_of[7], part), 71), part)
    prior_state = bell_draw(part_splits[4], (QUERY_SEQUENCES, ATTENDER_NUMBER, HD, HD), 1.0, 6.0, ((0, 8), (1, 16)), jnp.float32)
    lengths = uneven_parts(part_splits[5], QUERY_SEQUENCES, QUERY_SEQUENCES * CLOSING_TOKENS // 2 + CLOSING_TOKENS // 2, CLOSING_TOKENS, 2).astype(jnp.int32)
    owners_keys = jax.random.split(jax.random.fold_in(part_splits[6], 1), QUERY_SEQUENCES // REQ_DEV)
    owners_turns = jax.random.permutation(jax.random.fold_in(part_splits[6], 3), QUERY_SEQUENCES // REQ_DEV)
    owners = jax.vmap(lambda own, number: routed_block(jax.random.fold_in(part_splits[6], 2), own, number, REQ_DEV, N_DEC, 1, PAIR, 2))(owners_keys, owners_turns).reshape((QUERY_SEQUENCES, 1))
    return {"queries": queries, "keys": keys, "values": values, "log_decay": log_decay, "prior_state": prior_state, "lengths": lengths, "owners": owners}


def one_prompt(items):
    queries, keys, values, log_decay, prior_state, length = items
    tail_length, width = queries.shape
    head_count = log_decay.shape[1]
    block_size = width // head_count
    steps = jnp.arange(tail_length, dtype=jnp.int32)
    live = (steps < length).astype(jnp.float32)
    total = jnp.cumsum(log_decay * live[:, None], axis=0)
    qmat = queries.reshape(tail_length, head_count, block_size).astype(jnp.float32)
    kmat = keys.reshape(tail_length, head_count, block_size).astype(jnp.float32)
    value_matrix = values.reshape(tail_length, head_count, block_size).astype(jnp.float32)
    score = jnp.einsum("thc,shc->hts", qmat, kmat)
    lagged = total.T
    causal = steps[:, None] >= steps[None, :]
    gap = lagged[:, :, None] - lagged[:, None, :]
    fading = jnp.exp(jnp.where(causal[None], gap, -jnp.inf))
    decay_weight = (score * fading * live[None, None, :]).astype(jnp.bfloat16)
    inner_product = jnp.einsum("zep,pzf->ezf", decay_weight.astype(jnp.float32), value_matrix)
    carried = jnp.einsum("thc,hcd->thd", qmat, prior_state, precision=lax.Precision.HIGHEST) * jnp.exp(total)[:, :, None]
    output = ((inner_product + carried) * live[:, None, None]).astype(jnp.bfloat16).reshape(tail_length, width)
    last = total[-1]
    keep = jnp.exp(last[None, :] - total) * live[:, None]
    decayed_state = (kmat * keep[:, :, None]).astype(jnp.bfloat16)
    fresh_state = jnp.einsum("luk,luz->ukz", decayed_state.astype(jnp.float32), value_matrix)
    state = jnp.exp(last)[:, None, None] * prior_state + fresh_state
    return output, state


def reference(queries, keys, values, log_decay, prior_state, lengths, owners):
    prefill_out, states = lax.map(one_prompt, (queries, keys, values, log_decay, prior_state, lengths))
    own = owners[:, 0]
    count = own.shape[0]
    index = jnp.arange(count, dtype=jnp.int32)
    group = index // REQ_DEV
    same = (group[:, None] == group[None, :]) & (own[:, None] == own[None, :]) & (index[None, :] < index[:, None])
    rank = jnp.sum(same.astype(jnp.int32), axis=1).astype(jnp.int32)
    slot = (own * (N_PRE * PAIR) + group * PAIR + rank).astype(jnp.int32)
    decode_state = jnp.zeros((N_DEC * N_PRE * PAIR,) + states.shape[1:], jnp.float32).at[slot].set(states)
    return prefill_out, decode_state
```

```python
import jax
import jax.numpy as jnp
from jax import lax
from jax.experimental import pallas as pl
from jax.experimental.pallas import tpu as pltpu
from jax.sharding import PartitionSpec as P

HD = 128
ROWS = 8


def head_of(h):
    return slice(h * HD, (h + 1) * HD)


def column_sums(rate_rows):
    tokens = rate_rows.shape[1]
    row = lax.broadcasted_iota(jnp.int32, (tokens, tokens), 0)
    col = lax.broadcasted_iota(jnp.int32, (tokens, tokens), 1)
    lower = (col <= row).astype(jnp.float32)
    return lax.dot_general(
        lower, rate_rows, (((1,), (1,)), ((), ())),
        precision=lax.Precision.HIGHEST, preferred_element_type=jnp.float32,
    )


def row_sums(rate_rows):
    tokens = rate_rows.shape[1]
    row = lax.broadcasted_iota(jnp.int32, (tokens, tokens), 0)
    col = lax.broadcasted_iota(jnp.int32, (tokens, tokens), 1)
    upper = (row <= col).astype(jnp.float32)
    return lax.dot_general(
        rate_rows, upper, (((1,), (0,)), ((), ())),
        precision=lax.Precision.HIGHEST, preferred_element_type=jnp.float32,
    )


def state_kernel(lengths_ref, k_ref, v_ref, ld_ref, prior_ref, *out_refs):
    r = pl.program_id(0)
    length = lengths_ref[r]
    heads, tokens = ld_ref.shape[1:]
    per = heads // len(out_refs)
    live_row = lax.broadcasted_iota(jnp.int32, (heads, tokens), 1) < length
    total = column_sums(jnp.where(live_row, ld_ref[0], 0.0))
    last = total[tokens - 1:tokens, :]
    live_col = lax.broadcasted_iota(jnp.int32, (tokens, heads), 0) < length
    keep = jnp.where(live_col, jnp.exp(last - total), 0.0)
    final = jnp.exp(last)
    for h in range(heads):
        k = k_ref[0, :, head_of(h)].astype(jnp.float32)
        decayed = (k * keep[:, h:h + 1]).astype(jnp.bfloat16)
        fresh = lax.dot_general(
            decayed, v_ref[0, :, head_of(h)], (((0,), (0,)), ((), ())),
            preferred_element_type=jnp.float32,
        )
        state = final[:, h:h + 1] * prior_ref[0, h] + fresh
        out_refs[h // per][:, 0, h % per] = state.reshape(HD // ROWS, ROWS, HD)


def span_states(lengths, keys, values, ld, prior, chunks):
    prompts, tokens, width = keys.shape
    heads = ld.shape[1]
    per = heads // chunks
    pieces = HD // ROWS
    return pl.pallas_call(
        state_kernel,
        grid_spec=pltpu.PrefetchScalarGridSpec(
            num_scalar_prefetch=1,
            grid=(prompts,),
            in_specs=[
                pl.BlockSpec((1, tokens, width), lambda r, s: (r, 0, 0)),
                pl.BlockSpec((1, tokens, width), lambda r, s: (r, 0, 0)),
                pl.BlockSpec((1, heads, tokens), lambda r, s: (r, 0, 0)),
                pl.BlockSpec((1, heads, HD, HD), lambda r, s: (r, 0, 0, 0)),
            ],
            out_specs=[
                pl.BlockSpec((pieces, 1, per, ROWS, HD), lambda r, s: (0, r, 0, 0, 0))
                for _ in range(chunks)
            ],
        ),
        out_shape=[
            jax.ShapeDtypeStruct((pieces, prompts, per, ROWS, HD), jnp.float32)
            for _ in range(chunks)
        ],
        compiler_params=pltpu.CompilerParams(vmem_limit_bytes=32 << 20),
        name="span_states",
    )(lengths, keys, values, ld, prior)


def output_kernel(lengths_ref, q_ref, k_ref, v_ref, ld_ref, prior_ref, out_ref):
    r = pl.program_id(0)
    length = lengths_ref[r]
    heads, tokens = ld_ref.shape[1:]
    live_row = lax.broadcasted_iota(jnp.int32, (heads, tokens), 1) < length
    rate = jnp.where(live_row, ld_ref[0], 0.0)
    total_col = column_sums(rate)
    total_row = row_sums(rate)
    grow = jnp.exp(total_col)
    row = lax.broadcasted_iota(jnp.int32, (tokens, tokens), 0)
    col = lax.broadcasted_iota(jnp.int32, (tokens, tokens), 1)
    seen = (col <= row) & (col < length)
    live_col = lax.broadcasted_iota(jnp.int32, (tokens, HD), 0) < length
    for h in range(heads):
        q = q_ref[0, :, head_of(h)]
        score = lax.dot_general(
            q, k_ref[0, :, head_of(h)], (((1,), (1,)), ((), ())),
            preferred_element_type=jnp.float32,
        )
        gap = jnp.where(seen, total_col[:, h:h + 1] - total_row[h:h + 1, :], -jnp.inf)
        weight = (score * jnp.exp(gap)).astype(jnp.bfloat16)
        inner = jnp.dot(weight, v_ref[0, :, head_of(h)], preferred_element_type=jnp.float32)
        prior = prior_ref[0, h]
        high = prior.astype(jnp.bfloat16)
        rest = prior - high.astype(jnp.float32)
        mid = rest.astype(jnp.bfloat16)
        low = (rest - mid.astype(jnp.float32)).astype(jnp.bfloat16)
        carried = jnp.dot(q, low, preferred_element_type=jnp.float32)
        carried = carried + jnp.dot(q, mid, preferred_element_type=jnp.float32)
        carried = carried + jnp.dot(q, high, preferred_element_type=jnp.float32)
        out = inner + carried * grow[:, h:h + 1]
        out_ref[0, :, head_of(h)] = jnp.where(live_col, out, 0.0).astype(jnp.bfloat16)


def span_output(lengths, queries, keys, values, ld, prior):
    prompts, tokens, width = keys.shape
    heads = ld.shape[1]
    span = pl.BlockSpec((1, tokens, width), lambda r, s: (r, 0, 0))
    return pl.pallas_call(
        output_kernel,
        grid_spec=pltpu.PrefetchScalarGridSpec(
            num_scalar_prefetch=1,
            grid=(prompts,),
            in_specs=[
                span, span, span,
                pl.BlockSpec((1, heads, tokens), lambda r, s: (r, 0, 0)),
                pl.BlockSpec((1, heads, HD, HD), lambda r, s: (r, 0, 0, 0)),
            ],
            out_specs=span,
        ),
        out_shape=jax.ShapeDtypeStruct((prompts, tokens, width), jnp.bfloat16),
        compiler_params=pltpu.CompilerParams(vmem_limit_bytes=32 << 20),
        cost_estimate=pl.CostEstimate(
            flops=2 * prompts * heads * tokens * HD * (2 * tokens + 3 * HD),
            bytes_accessed=8 * prompts * tokens * width + 4 * prompts * heads * HD * HD,
            transcendentals=prompts * heads * tokens * tokens,
        ),
        name="span_output",
    )(lengths, queries, keys, values, ld, prior)


def address_kernel(owners_ref, held_ref, out_ref, sem):
    groups, _, prompts = held_ref.shape[:3]

    def block(i):
        g = i // prompts
        r = i % prompts
        return pltpu.make_async_copy(
            held_ref.at[g, :, r], out_ref.at[owners_ref[i], g], sem
        )

    @pl.loop(0, groups * prompts)
    def _(i):
        block(i).start()

    pltpu.make_async_copy(held_ref, held_ref, sem).wait()


def address(all_owners, held, count):
    groups, halves, prompts, per = held.shape[:4]
    return pl.pallas_call(
        address_kernel,
        in_specs=[
            pl.BlockSpec(memory_space=pltpu.SMEM),
            pl.BlockSpec(memory_space=pl.ANY),
        ],
        out_specs=pl.BlockSpec(memory_space=pl.ANY),
        out_shape=jax.ShapeDtypeStruct((count, groups, halves, per, ROWS, HD), jnp.float32),
        scratch_shapes=[pltpu.SemaphoreType.DMA],
        name="address",
    )(all_owners, held)


def place_kernel(present_ref, *refs):
    out_ref = refs[-1]
    g = pl.program_id(0)
    here = present_ref[g] > 0
    chunks = len(refs) - 1

    @pl.when(here)
    def _():
        for c in range(chunks):
            pieces, _, halves, per = refs[c].shape[:4]
            for b in range(halves):
                for e in range(per):
                    h = (b * chunks + c) * per + e
                    out_ref[0, h] = refs[c][:, 0, b, e].reshape(pieces * ROWS, HD)

    @pl.when(jnp.logical_not(here))
    def _():
        out_ref[...] = jnp.zeros_like(out_ref)


def place(present, parts):
    pieces, groups, halves, per = parts[0].shape[:4]
    heads = halves * per * len(parts)
    return pl.pallas_call(
        place_kernel,
        grid_spec=pltpu.PrefetchScalarGridSpec(
            num_scalar_prefetch=1,
            grid=(groups,),
            in_specs=[
                pl.BlockSpec((pieces, 1, halves, per, ROWS, HD), lambda g, s: (0, g, 0, 0, 0, 0))
                for _ in parts
            ],
            out_specs=pl.BlockSpec((1, heads, HD, HD), lambda g, s: (g, 0, 0, 0)),
        ),
        out_shape=jax.ShapeDtypeStruct((groups, heads, HD, HD), jnp.float32),
        compiler_params=pltpu.CompilerParams(vmem_limit_bytes=32 << 20),
        name="place",
    )(present, *parts)


CHUNKS = 1


def shards(queries, keys, values, log_decay, prior_state, lengths, owners):
    n_pre = lax.axis_size("pre")
    n_dec = lax.axis_size("dec")
    prompts = keys.shape[0]
    ld = jnp.swapaxes(log_decay, 1, 2)
    all_owners = lax.all_gather(owners[:, 0], "pre", axis=0, tiled=True)
    mine = lax.axis_index("dec")
    present = jnp.any(all_owners.reshape(n_pre, prompts) == mine, axis=1).astype(jnp.int32)
    states = span_states(lengths, keys, values, ld, prior_state, CHUNKS)
    parts = []
    for piece in states:
        mixed = lax.all_to_all(piece, "dec", split_axis=0, concat_axis=0, tiled=True)
        held = lax.all_to_all(mixed, "pre", split_axis=0, concat_axis=0, tiled=True)
        held = held.reshape((n_pre, n_dec // n_pre) + held.shape[1:])
        sent = address(all_owners, held, n_dec)
        parts.append(lax.all_to_all(sent, "dec", split_axis=0, concat_axis=0, tiled=True))
    prefill_out = span_output(lengths, queries, keys, values, ld, prior_state)
    decode_state = place(present, parts)
    return prefill_out, decode_state


def solution(mesh):
    placed = (
        P(("rep", "pre"), None, "dec"),
        P(("rep", "pre"), None, "dec"),
        P(("rep", "pre"), None, "dec"),
        P(("rep", "pre"), None, "dec"),
        P(("rep", "pre"), "dec", None, None),
        P(("rep", "pre")),
        P(("rep", "pre"), None),
    )
    return jax.shard_map(
        shards,
        mesh=mesh,
        in_specs=placed,
        out_specs=(P(("rep", "pre"), None, "dec"), P(("rep", "dec"), "pre", None, None)),
        check_vma=False,
    )
```

```python
import functools

import jax
import jax.numpy as jnp
from jax import lax
from jax.experimental import pallas as pl
from jax.experimental.pallas import tpu as pltpu
from jax.sharding import PartitionSpec as P

HD = 128
ROWS = 8
VMEM = 56 << 20
SHIFTS = ((0, 1, 7, 2), (6, 3, 5, 4))


def head_of(h):
    return slice(h * HD, (h + 1) * HD)


def column_sums(rate_rows):
    tokens = rate_rows.shape[1]
    row = lax.broadcasted_iota(jnp.int32, (tokens, tokens), 0)
    col = lax.broadcasted_iota(jnp.int32, (tokens, tokens), 1)
    lower = (col <= row).astype(jnp.float32)
    return lax.dot_general(
        lower, rate_rows, (((1,), (1,)), ((), ())),
        precision=lax.Precision.HIGHEST, preferred_element_type=jnp.float32,
    )


def row_sums(rate_rows):
    tokens = rate_rows.shape[1]
    row = lax.broadcasted_iota(jnp.int32, (tokens, tokens), 0)
    col = lax.broadcasted_iota(jnp.int32, (tokens, tokens), 1)
    upper = (row <= col).astype(jnp.float32)
    return lax.dot_general(
        rate_rows, upper, (((1,), (0,)), ((), ())),
        precision=lax.Precision.HIGHEST, preferred_element_type=jnp.float32,
    )


def state_kernel(lengths_ref, k_ref, v_ref, ld_ref, prior_ref, owners_ref, out_ref):
    r = pl.program_id(0)
    length = lengths_ref[r]
    heads, tokens = ld_ref.shape[1:]
    live_row = lax.broadcasted_iota(jnp.int32, (heads, tokens), 1) < length
    total = column_sums(jnp.where(live_row, ld_ref[0], 0.0))
    last = total[tokens - 1:tokens, :]
    live_col = lax.broadcasted_iota(jnp.int32, (tokens, heads), 0) < length
    keep = jnp.where(live_col, jnp.exp(last - total), 0.0)
    final = jnp.exp(last)
    for h in range(heads):
        k = k_ref[0, :, head_of(h)].astype(jnp.float32)
        decayed = (k * keep[:, h:h + 1]).astype(jnp.bfloat16)
        fresh = lax.dot_general(
            decayed, v_ref[0, :, head_of(h)], (((0,), (0,)), ((), ())),
            preferred_element_type=jnp.float32,
        )
        state = final[:, h:h + 1] * prior_ref[0, h] + fresh
        out_ref[:, r * heads + h] = state.reshape(HD // ROWS, ROWS, HD)

    @pl.when(r == 0)
    def _():
        named = jnp.broadcast_to(owners_ref[...], out_ref.shape[2:])
        for j in range(out_ref.shape[0]):
            out_ref[j, out_ref.shape[1] - 1] = named


def span_states(lengths, keys, values, ld, prior, owners):
    prompts, tokens, width = keys.shape
    heads = ld.shape[1]
    pieces = HD // ROWS
    named = jnp.pad(owners.astype(jnp.float32), ((0, ROWS - prompts), (0, 0)))
    shape = (pieces, prompts * heads + 1, ROWS, HD)
    return pl.pallas_call(
        state_kernel,
        grid_spec=pltpu.PrefetchScalarGridSpec(
            num_scalar_prefetch=1,
            grid=(prompts,),
            in_specs=[
                pl.BlockSpec((1, tokens, width), lambda r, s: (r, 0, 0)),
                pl.BlockSpec((1, tokens, width), lambda r, s: (r, 0, 0)),
                pl.BlockSpec((1, heads, tokens), lambda r, s: (r, 0, 0)),
                pl.BlockSpec((1, heads, HD, HD), lambda r, s: (r, 0, 0, 0)),
                pl.BlockSpec((ROWS, 1), lambda r, s: (0, 0)),
            ],
            out_specs=pl.BlockSpec(shape, lambda r, s: (0, 0, 0, 0)),
        ),
        out_shape=jax.ShapeDtypeStruct(shape, jnp.float32),
        compiler_params=pltpu.CompilerParams(vmem_limit_bytes=VMEM),
        name="span_states",
    )(lengths, keys, values, ld, prior, named)


def output_kernel(lengths_ref, q_ref, k_ref, v_ref, ld_ref, prior_ref, out_ref):
    r = pl.program_id(0)
    length = lengths_ref[r]
    heads, tokens = ld_ref.shape[1:]
    live_row = lax.broadcasted_iota(jnp.int32, (heads, tokens), 1) < length
    rate = jnp.where(live_row, ld_ref[0], 0.0)
    total_col = column_sums(rate)
    total_row = row_sums(rate)
    grow = jnp.exp(total_col)
    row = lax.broadcasted_iota(jnp.int32, (tokens, tokens), 0)
    col = lax.broadcasted_iota(jnp.int32, (tokens, tokens), 1)
    seen = (col <= row) & (col < length)
    live_col = lax.broadcasted_iota(jnp.int32, (tokens, HD), 0) < length
    for h in range(heads):
        q = q_ref[0, :, head_of(h)]
        score = lax.dot_general(
            q, k_ref[0, :, head_of(h)], (((1,), (1,)), ((), ())),
            preferred_element_type=jnp.float32,
        )
        gap = jnp.where(seen, total_col[:, h:h + 1] - total_row[h:h + 1, :], -jnp.inf)
        weight = (score * jnp.exp(gap)).astype(jnp.bfloat16)
        inner = jnp.dot(weight, v_ref[0, :, head_of(h)], preferred_element_type=jnp.float32)
        prior = prior_ref[0, h]
        high = prior.astype(jnp.bfloat16)
        rest = prior - high.astype(jnp.float32)
        mid = rest.astype(jnp.bfloat16)
        low = (rest - mid.astype(jnp.float32)).astype(jnp.bfloat16)
        carried = jnp.dot(q, low, preferred_element_type=jnp.float32)
        carried = carried + jnp.dot(q, mid, preferred_element_type=jnp.float32)
        carried = carried + jnp.dot(q, high, preferred_element_type=jnp.float32)
        out = inner + carried * grow[:, h:h + 1]
        out_ref[0, :, head_of(h)] = jnp.where(live_col, out, 0.0).astype(jnp.bfloat16)


def span_output(lengths, queries, keys, values, ld, prior):
    prompts, tokens, width = keys.shape
    heads = ld.shape[1]
    span = pl.BlockSpec((1, tokens, width), lambda r, s: (r, 0, 0))
    return pl.pallas_call(
        output_kernel,
        grid_spec=pltpu.PrefetchScalarGridSpec(
            num_scalar_prefetch=1,
            grid=(prompts,),
            in_specs=[
                span, span, span,
                pl.BlockSpec((1, heads, tokens), lambda r, s: (r, 0, 0)),
                pl.BlockSpec((1, heads, HD, HD), lambda r, s: (r, 0, 0, 0)),
            ],
            out_specs=span,
        ),
        out_shape=jax.ShapeDtypeStruct((prompts, tokens, width), jnp.bfloat16),
        compiler_params=pltpu.CompilerParams(vmem_limit_bytes=VMEM),
        cost_estimate=pl.CostEstimate(
            flops=2 * prompts * heads * tokens * HD * (2 * tokens + 3 * HD),
            bytes_accessed=8 * prompts * tokens * width + 4 * prompts * heads * HD * HD,
            transcendentals=prompts * heads * tokens * tokens,
        ),
        name="span_output",
    )(lengths, queries, keys, values, ld, prior)


def address_kernel(slots, *refs):
    held = refs[:slots]
    out_ref, names, name_sems, sems = refs[slots:]
    per = out_ref.shape[3]
    rows = held[0].shape[1] - 1
    for j in range(slots):
        pltpu.make_async_copy(held[j].at[0, rows], names.at[j], name_sems.at[j]).start()
    for j in range(slots):
        pltpu.make_async_copy(held[j].at[0, rows], names.at[j], name_sems.at[j]).wait()
        for r in range(rows // per):
            owner = names[j, r, 0].astype(jnp.int32)
            pltpu.make_async_copy(
                held[j].at[:, pl.ds(r * per, per)], out_ref.at[owner, j], sems.at[j]
            ).start()
    for j in range(slots):
        sent = held[j].at[:, pl.ds(0, rows)]
        pltpu.make_async_copy(sent, sent, sems.at[j]).wait()


def address(held, count, heads):
    slots = len(held)
    halves = held[0].shape[0]
    return pl.pallas_call(
        functools.partial(address_kernel, slots),
        in_specs=[pl.BlockSpec(memory_space=pltpu.VMEM) for _ in held],
        out_specs=pl.BlockSpec(memory_space=pl.ANY),
        out_shape=jax.ShapeDtypeStruct((count, slots, halves, heads, ROWS, HD), jnp.float32),
        scratch_shapes=[
            pltpu.SMEM((slots, ROWS, HD), jnp.float32),
            pltpu.SemaphoreType.DMA((slots,)),
            pltpu.SemaphoreType.DMA((slots,)),
        ],
        compiler_params=pltpu.CompilerParams(vmem_limit_bytes=VMEM),
        name="address",
    )(*held)


def place_kernel(groups_ref, present_ref, got_ref, *refs):
    out_ref, got, placed, in_sems, out_sems = refs[-5:]
    pieces, slots, halves, per = got_ref.shape[:4]

    def fetch(j):
        return pltpu.make_async_copy(got_ref.at[:, j], got.at[j], in_sems.at[j])

    def store(j):
        return pltpu.make_async_copy(placed.at[j], out_ref.at[groups_ref[j]], out_sems.at[j])

    for j in range(slots):
        @pl.when(present_ref[j] > 0)
        def _():
            fetch(j).start()

    for j in range(slots):
        @pl.when(present_ref[j] == 0)
        def _():
            placed[j] = jnp.zeros(placed.shape[1:], jnp.float32)

        @pl.when(present_ref[j] > 0)
        def _():
            fetch(j).wait()
            for b in range(halves):
                for e in range(per):
                    placed[j, b * per + e] = got[j, :, b, e].reshape(pieces * ROWS, HD)

        store(j).start()
    for j in range(slots):
        store(j).wait()


def place(groups, present, got, n_groups, out=None):
    pieces, slots, halves, per = got.shape[:4]
    heads = halves * per
    smem = pl.BlockSpec(memory_space=pltpu.SMEM)
    hbm = pl.BlockSpec(memory_space=pl.ANY)
    given = [groups, present, got] + ([] if out is None else [out])
    return pl.pallas_call(
        place_kernel,
        in_specs=[smem, smem, hbm] + ([] if out is None else [hbm]),
        out_specs=hbm,
        out_shape=jax.ShapeDtypeStruct((n_groups, heads, HD, HD), jnp.float32),
        input_output_aliases={} if out is None else {3: 0},
        scratch_shapes=[
            pltpu.VMEM((slots, pieces, halves, per, ROWS, HD), jnp.float32),
            pltpu.VMEM((slots, heads, HD, HD), jnp.float32),
            pltpu.SemaphoreType.DMA((slots,)),
            pltpu.SemaphoreType.DMA((slots,)),
        ],
        compiler_params=pltpu.CompilerParams(vmem_limit_bytes=VMEM),
        name="place",
    )(*given)


def shifted(mixed, shift, n_pre):
    halves = mixed.shape[0] // n_pre
    goal = lax.rem(lax.axis_index("pre") + shift, n_pre)
    part = lax.dynamic_slice_in_dim(mixed, goal * halves, halves, 0)
    if shift == 0:
        return part
    return lax.ppermute(part, "pre", [(i, (i + shift) % n_pre) for i in range(n_pre)])


def shards(queries, keys, values, log_decay, prior_state, lengths, owners):
    n_pre = lax.axis_size("pre")
    n_dec = lax.axis_size("dec")
    prompts, heads = prior_state.shape[:2]
    me_pre, me_dec = lax.axis_index("pre"), lax.axis_index("dec")
    ld = jnp.swapaxes(log_decay, 1, 2)
    states = span_states(lengths, keys, values, ld, prior_state, owners)
    mixed = lax.all_to_all(states, "dec", split_axis=0, concat_axis=0, tiled=True)
    held = {m: shifted(mixed, m, n_pre) for batch in SHIFTS for m in batch}
    decode_state = None
    for batch in SHIFTS:
        blocks = [held[m] for m in batch]
        sent = address(blocks, n_dec, heads)
        got = lax.all_to_all(sent, "dec", split_axis=0, concat_axis=0, tiled=True)
        named = jnp.stack([x[0, -1, :prompts, 0] for x in blocks]).astype(jnp.int32)
        present = jnp.any(named == me_dec, axis=1).astype(jnp.int32)
        groups = lax.rem(me_pre + n_pre - jnp.array(batch, jnp.int32), n_pre)
        decode_state = place(groups, present, got, n_pre, decode_state)
    prefill_out = span_output(lengths, queries, keys, values, ld, prior_state)
    return prefill_out, decode_state


def solution(mesh):
    placed = (
        P(("rep", "pre"), None, "dec"),
        P(("rep", "pre"), None, "dec"),
        P(("rep", "pre"), None, "dec"),
        P(("rep", "pre"), None, "dec"),
        P(("rep", "pre"), "dec", None, None),
        P(("rep", "pre")),
        P(("rep", "pre"), None),
    )
    return jax.shard_map(
        shards,
        mesh=mesh,
        in_specs=placed,
        out_specs=(P(("rep", "pre"), None, "dec"), P(("rep", "dec"), "pre", None, None)),
        check_vma=False,
    )
```

```python
import functools

import jax
import jax.numpy as jnp
from jax import lax
from jax.experimental import pallas as pl
from jax.experimental.pallas import tpu as pltpu
from jax.sharding import PartitionSpec as P

HD = 128
ROWS = 8
VMEM = 56 << 20
PARTS = 2
STEPS = 2
ORDER = (0, 1, 7, 2, 6, 3, 5, 4)
LATE = 5
FIRST = 0


def head_of(h):
    return slice(h * HD, (h + 1) * HD)


def column_sums(rate_rows):
    tokens = rate_rows.shape[1]
    row = lax.broadcasted_iota(jnp.int32, (tokens, tokens), 0)
    col = lax.broadcasted_iota(jnp.int32, (tokens, tokens), 1)
    lower = (col <= row).astype(jnp.float32)
    return lax.dot_general(
        lower, rate_rows, (((1,), (1,)), ((), ())),
        precision=lax.Precision.HIGHEST, preferred_element_type=jnp.float32,
    )


def row_sums(rate_rows):
    tokens = rate_rows.shape[1]
    row = lax.broadcasted_iota(jnp.int32, (tokens, tokens), 0)
    col = lax.broadcasted_iota(jnp.int32, (tokens, tokens), 1)
    upper = (row <= col).astype(jnp.float32)
    return lax.dot_general(
        rate_rows, upper, (((1,), (0,)), ((), ())),
        precision=lax.Precision.HIGHEST, preferred_element_type=jnp.float32,
    )


def split_three(x):
    high = x.astype(jnp.bfloat16).astype(jnp.float32)
    rest = x - high
    mid = rest.astype(jnp.bfloat16).astype(jnp.float32)
    return high, mid, rest - mid


def final_states(length, p, k_ref, v_ref, rate, prior_ref, upper):
    heads, tokens = rate.shape
    live = lax.broadcasted_iota(jnp.int32, (heads, tokens), 1) < length
    terms = jnp.concatenate(split_three(jnp.where(live, rate, 0.0)), axis=0).astype(jnp.bfloat16)
    sums = jnp.dot(terms, upper, preferred_element_type=jnp.float32)
    total = sums[2 * heads:] + sums[heads:2 * heads] + sums[:heads]
    last = total[:, tokens - 1:tokens]
    keep = jnp.where(live, jnp.exp(last - total), 0.0)
    final = jnp.exp(last)
    states = []
    for h in range(heads):
        k = k_ref[p, :, head_of(h)].astype(jnp.float32).T
        decayed = (k * keep[h:h + 1, :]).astype(jnp.bfloat16)
        fresh = jnp.dot(decayed, v_ref[p, :, head_of(h)], preferred_element_type=jnp.float32)
        states.append(final[h:h + 1, :] * prior_ref[p, h] + fresh)
    return states


def fill_upper(upper_ref):
    row = lax.broadcasted_iota(jnp.int32, upper_ref.shape, 0)
    col = lax.broadcasted_iota(jnp.int32, upper_ref.shape, 1)
    upper_ref[...] = jnp.where(row <= col, 1.0, 0.0).astype(jnp.bfloat16)


def mixing_kernel(first, lengths_ref, owners_ref, k_ref, v_ref, ld_ref, prior_ref, out_ref, upper_ref):
    step = pl.program_id(0)
    each, heads = prior_ref.shape[:2]

    @pl.when(step == 0)
    def _():
        fill_upper(upper_ref)
        row = lax.broadcasted_iota(jnp.int32, out_ref.shape[2:], 0)
        named = jnp.zeros(out_ref.shape[2:], jnp.int32)
        for i in range(owners_ref.shape[0]):
            named = jnp.where(row == i, owners_ref[i], named)
        for j in range(out_ref.shape[0]):
            out_ref[j, out_ref.shape[1] - 1] = named.astype(jnp.float32)

    for p in range(each):
        r = step * each + p
        rate = ld_ref[p, first:first + heads]
        states = final_states(lengths_ref[r], p, k_ref, v_ref, rate, prior_ref, upper_ref[...])
        for h in range(heads):
            out_ref[:, r * heads + h] = states[h].reshape(HD // ROWS, ROWS, HD)


def owner_kernel(first, lengths_ref, owners_ref, k_ref, v_ref, ld_ref, prior_ref, out_ref, upper_ref):
    step = pl.program_id(0)
    each, heads = prior_ref.shape[:2]

    @pl.when(step == 0)
    def _():
        fill_upper(upper_ref)

    for p in range(each):
        r = step * each + p
        rate = ld_ref[p, first:first + heads]
        states = final_states(lengths_ref[r], p, k_ref, v_ref, rate, prior_ref, upper_ref[...])
        for h in range(heads):
            out_ref[owners_ref[r], h] = states[h]


def span_states(mixing, first, per, lengths, owned, keys, values, ld, prior, count):
    prompts, tokens, width = keys.shape
    heads = ld.shape[1]
    each = prompts // STEPS
    block = first // per
    if mixing:
        shape = (HD // ROWS, prompts * per + 1, ROWS, HD)
    else:
        shape = (count, per, HD, HD)
    return pl.pallas_call(
        functools.partial(mixing_kernel if mixing else owner_kernel, first),
        grid_spec=pltpu.PrefetchScalarGridSpec(
            num_scalar_prefetch=2,
            grid=(STEPS,),
            in_specs=[
                pl.BlockSpec((each, tokens, per * HD), lambda r, s, o: (r, 0, block)),
                pl.BlockSpec((each, tokens, per * HD), lambda r, s, o: (r, 0, block)),
                pl.BlockSpec((each, heads, tokens), lambda r, s, o: (r, 0, 0)),
                pl.BlockSpec((each, per, HD, HD), lambda r, s, o: (r, block, 0, 0)),
            ],
            out_specs=pl.BlockSpec(shape, lambda r, s, o: (0, 0, 0, 0)),
            scratch_shapes=[pltpu.VMEM((tokens, tokens), jnp.bfloat16)],
        ),
        out_shape=jax.ShapeDtypeStruct(shape, jnp.float32),
        compiler_params=pltpu.CompilerParams(vmem_limit_bytes=VMEM),
        cost_estimate=pl.CostEstimate(
            flops=2 * prompts * per * tokens * HD * HD,
            bytes_accessed=4 * prompts * tokens * per * HD + 8 * prompts * per * HD * HD,
            transcendentals=prompts * per * tokens,
        ),
        name="span_states",
    )(lengths, owned, keys, values, ld, prior)


def output_kernel(lengths_ref, q_ref, k_ref, v_ref, ld_ref, prior_ref, out_ref):
    r = pl.program_id(0)
    length = lengths_ref[r]
    heads, tokens = ld_ref.shape[1:]
    live_row = lax.broadcasted_iota(jnp.int32, (heads, tokens), 1) < length
    rate = jnp.where(live_row, ld_ref[0], 0.0)
    total_col = column_sums(rate)
    total_row = row_sums(rate)
    grow = jnp.exp(total_col)
    row = lax.broadcasted_iota(jnp.int32, (tokens, tokens), 0)
    col = lax.broadcasted_iota(jnp.int32, (tokens, tokens), 1)
    seen = (col <= row) & (col < length)
    live_col = lax.broadcasted_iota(jnp.int32, (tokens, HD), 0) < length
    for h in range(heads):
        q = q_ref[0, :, head_of(h)]
        score = lax.dot_general(
            q, k_ref[0, :, head_of(h)], (((1,), (1,)), ((), ())),
            preferred_element_type=jnp.float32,
        )
        gap = jnp.where(seen, total_col[:, h:h + 1] - total_row[h:h + 1, :], -jnp.inf)
        weight = (score * jnp.exp(gap)).astype(jnp.bfloat16)
        inner = jnp.dot(weight, v_ref[0, :, head_of(h)], preferred_element_type=jnp.float32)
        prior = prior_ref[0, h]
        high = prior.astype(jnp.bfloat16)
        rest = prior - high.astype(jnp.float32)
        mid = rest.astype(jnp.bfloat16)
        low = (rest - mid.astype(jnp.float32)).astype(jnp.bfloat16)
        carried = jnp.dot(q, low, preferred_element_type=jnp.float32)
        carried = carried + jnp.dot(q, mid, preferred_element_type=jnp.float32)
        carried = carried + jnp.dot(q, high, preferred_element_type=jnp.float32)
        out = inner + carried * grow[:, h:h + 1]
        out_ref[0, :, head_of(h)] = jnp.where(live_col, out, 0.0).astype(jnp.bfloat16)


def span_output(lengths, queries, keys, values, ld, prior):
    prompts, tokens, width = keys.shape
    heads = ld.shape[1]
    span = pl.BlockSpec((1, tokens, width), lambda r, s: (r, 0, 0))
    return pl.pallas_call(
        output_kernel,
        grid_spec=pltpu.PrefetchScalarGridSpec(
            num_scalar_prefetch=1,
            grid=(prompts,),
            in_specs=[
                span, span, span,
                pl.BlockSpec((1, heads, tokens), lambda r, s: (r, 0, 0)),
                pl.BlockSpec((1, heads, HD, HD), lambda r, s: (r, 0, 0, 0)),
            ],
            out_specs=span,
        ),
        out_shape=jax.ShapeDtypeStruct((prompts, tokens, width), jnp.bfloat16),
        compiler_params=pltpu.CompilerParams(vmem_limit_bytes=VMEM),
        cost_estimate=pl.CostEstimate(
            flops=2 * prompts * heads * tokens * HD * (2 * tokens + 3 * HD),
            bytes_accessed=8 * prompts * tokens * width + 4 * prompts * heads * HD * HD,
            transcendentals=prompts * heads * tokens * tokens,
        ),
        name="span_output",
    )(lengths, queries, keys, values, ld, prior)


def address_kernel(slots, n_pre, where_ref, *refs):
    held = refs[:slots]
    out_ref, groups_ref, present_ref, names, name_sems, sems = refs[slots:]
    per = out_ref.shape[3]
    rows = held[0].shape[1] - 1

    def fetch(j):
        return pltpu.make_async_copy(held[j].at[0, rows], names.at[j], name_sems.at[j])

    for j in range(slots):
        fetch(j).start()
    for j in range(slots):
        fetch(j).wait()
        groups_ref[j] = lax.rem(where_ref[0] + n_pre - ORDER[j], n_pre)
        present = jnp.int32(0)
        for r in range(rows // per):
            owner = names[j, r, 0].astype(jnp.int32)
            present = jnp.where(owner == where_ref[1], 1, present)
            pltpu.make_async_copy(
                held[j].at[:, pl.ds(r * per, per)], out_ref.at[owner, j], sems.at[j]
            ).start()
        present_ref[j] = present
    for j in range(slots):
        sent = held[j].at[:, pl.ds(0, rows)]
        pltpu.make_async_copy(sent, sent, sems.at[j]).wait()


def address(where, held, count, per):
    slots = len(held)
    halves = held[0].shape[0]
    smem = pl.BlockSpec(memory_space=pltpu.SMEM)
    return pl.pallas_call(
        functools.partial(address_kernel, slots, len(ORDER)),
        in_specs=[smem] + [pl.BlockSpec(memory_space=pltpu.VMEM) for _ in held],
        out_specs=[pl.BlockSpec(memory_space=pl.ANY), smem, smem],
        out_shape=[
            jax.ShapeDtypeStruct((count, slots, halves, per, ROWS, HD), jnp.float32),
            jax.ShapeDtypeStruct((slots,), jnp.int32),
            jax.ShapeDtypeStruct((slots,), jnp.int32),
        ],
        scratch_shapes=[
            pltpu.SMEM((slots, ROWS, HD), jnp.float32),
            pltpu.SemaphoreType.DMA((slots,)),
            pltpu.SemaphoreType.DMA((slots,)),
        ],
        compiler_params=pltpu.CompilerParams(vmem_limit_bytes=VMEM),
        name="address",
    )(where, *held)


def place_rows_kernel(groups_ref, present_ref, got_ref, out_ref, got, placed, in_sems, out_sems):
    pieces, slots, halves, per = got_ref.shape[:4]

    def fetch(j):
        return pltpu.make_async_copy(got_ref.at[:, j], got.at[j], in_sems.at[j])

    def store(j):
        return pltpu.make_async_copy(placed.at[j], out_ref.at[groups_ref[j], :, 0], out_sems.at[j])

    for j in range(slots):
        @pl.when(present_ref[j] > 0)
        def _():
            fetch(j).start()

    for j in range(slots):
        @pl.when(present_ref[j] == 0)
        def _():
            placed[j] = jnp.zeros(placed.shape[1:], jnp.float32)

        @pl.when(present_ref[j] > 0)
        def _():
            fetch(j).wait()
            for b in range(halves):
                for e in range(per):
                    placed[j, b, e] = got[j, :, b, e].reshape(pieces * ROWS, HD)

        store(j).start()
    for j in range(slots):
        store(j).wait()


def place_rows(groups, present, got, n_groups):
    pieces, slots, halves, per = got.shape[:4]
    smem = pl.BlockSpec(memory_space=pltpu.SMEM)
    hbm = pl.BlockSpec(memory_space=pl.ANY)
    return pl.pallas_call(
        place_rows_kernel,
        in_specs=[smem, smem, hbm],
        out_specs=hbm,
        out_shape=jax.ShapeDtypeStruct((n_groups, halves, PARTS, per, HD, HD), jnp.float32),
        scratch_shapes=[
            pltpu.VMEM((slots, pieces, halves, per, ROWS, HD), jnp.float32),
            pltpu.VMEM((slots, halves, per, HD, HD), jnp.float32),
            pltpu.SemaphoreType.DMA((slots,)),
            pltpu.SemaphoreType.DMA((slots,)),
        ],
        compiler_params=pltpu.CompilerParams(vmem_limit_bytes=VMEM),
        name="place_rows",
    )(groups, present, got)


def place_blocks_kernel(first, slots, groups_ref, present_ref, *refs):
    got = refs[:slots]
    out_ref, empty, sems = refs[slots + 1:]
    empty[...] = jnp.zeros(empty.shape, jnp.float32)
    for j in range(slots):
        target = out_ref.at[groups_ref[first + j], :, 1]

        @pl.when(present_ref[first + j] > 0)
        def _():
            pltpu.make_async_copy(got[j], target, sems.at[j]).start()

        @pl.when(present_ref[first + j] == 0)
        def _():
            pltpu.make_async_copy(empty, target, sems.at[j]).start()

    for j in range(slots):
        pltpu.make_async_copy(empty, empty, sems.at[j]).wait()


def place_blocks(first, groups, present, got, out):
    slots = len(got)
    smem = pl.BlockSpec(memory_space=pltpu.SMEM)
    hbm = pl.BlockSpec(memory_space=pl.ANY)
    return pl.pallas_call(
        functools.partial(place_blocks_kernel, first, slots),
        in_specs=[smem, smem] + [pl.BlockSpec(memory_space=pltpu.VMEM)] * slots + [hbm],
        out_specs=hbm,
        out_shape=jax.ShapeDtypeStruct(out.shape, jnp.float32),
        input_output_aliases={2 + slots: 0},
        scratch_shapes=[
            pltpu.VMEM(got[0].shape, jnp.float32),
            pltpu.SemaphoreType.DMA((slots,)),
        ],
        compiler_params=pltpu.CompilerParams(vmem_limit_bytes=VMEM),
        name="place_blocks",
    )(groups, present, *got, out)


def shifted(mixed, shift, n_pre):
    halves = mixed.shape[0] // n_pre
    goal = lax.rem(lax.axis_index("pre") + shift, n_pre)
    part = lax.dynamic_slice_in_dim(mixed, goal * halves, halves, 0)
    if shift == 0:
        return part
    return lax.ppermute(part, "pre", [(i, (i + shift) % n_pre) for i in range(n_pre)])


def over_dec(x):
    return lax.all_to_all(x, "dec", split_axis=0, concat_axis=0, tiled=True)


def shards(queries, keys, values, log_decay, prior_state, lengths, owners):
    n_pre = lax.axis_size("pre")
    n_dec = lax.axis_size("dec")
    heads = prior_state.shape[1]
    ld = jnp.swapaxes(log_decay, 1, 2)
    spans = (lengths, owners[:, 0], keys, values, ld, prior_state, n_dec)
    per = heads // PARTS
    where = jnp.stack([lax.axis_index("pre"), lax.axis_index("dec")]).astype(jnp.int32)
    mixed = over_dec(span_states(True, 0, per, *spans))
    named = span_states(False, per, per, *spans)
    prefill_out = span_output(lengths, queries, keys, values, ld, prior_state)
    named, mixed, prefill_out, where = lax.optimization_barrier((named, mixed, prefill_out, where))
    owned = over_dec(named)
    held = [shifted(mixed, m, n_pre) for m in ORDER]
    blocks = [shifted(owned, m, n_pre) for m in ORDER]
    held, blocks[:FIRST] = lax.optimization_barrier((held, blocks[:FIRST]))
    sent, groups, present = address(where, held, n_dec, per)
    got = over_dec(sent)
    decode_state = place_rows(groups, present, got, n_pre)
    decode_state = place_blocks(0, groups, present, blocks[:LATE], decode_state)
    decode_state = place_blocks(LATE, groups, present, blocks[LATE:], decode_state)
    return prefill_out, decode_state.reshape(n_pre, -1, HD, HD)


def solution(mesh):
    placed = (
        P(("rep", "pre"), None, "dec"),
        P(("rep", "pre"), None, "dec"),
        P(("rep", "pre"), None, "dec"),
        P(("rep", "pre"), None, "dec"),
        P(("rep", "pre"), "dec", None, None),
        P(("rep", "pre")),
        P(("rep", "pre"), None),
    )
    return jax.shard_map(
        shards,
        mesh=mesh,
        in_specs=placed,
        out_specs=(P(("rep", "pre"), None, "dec"), P(("rep", "dec"), "pre", None, None)),
        check_vma=False,
    )
```

```python
import functools

import jax
import jax.numpy as jnp
from jax import lax
from jax.experimental import pallas as pl
from jax.experimental.pallas import tpu as pltpu
from jax.sharding import PartitionSpec as P

HD = 128
ROWS = 8
VMEM = 56 << 20
PARTS = 2
STEPS = 2
ORDER = (0, 1, 7, 2, 6, 3, 5, 4)
LATE = 5
FIRST = 0


def head_of(h):
    return slice(h * HD, (h + 1) * HD)


def column_sums(rate_rows):
    tokens = rate_rows.shape[1]
    row = lax.broadcasted_iota(jnp.int32, (tokens, tokens), 0)
    col = lax.broadcasted_iota(jnp.int32, (tokens, tokens), 1)
    lower = (col <= row).astype(jnp.float32)
    return lax.dot_general(
        lower, rate_rows, (((1,), (1,)), ((), ())),
        precision=lax.Precision.HIGHEST, preferred_element_type=jnp.float32,
    )


def row_sums(rate_rows):
    tokens = rate_rows.shape[1]
    row = lax.broadcasted_iota(jnp.int32, (tokens, tokens), 0)
    col = lax.broadcasted_iota(jnp.int32, (tokens, tokens), 1)
    upper = (row <= col).astype(jnp.float32)
    return lax.dot_general(
        rate_rows, upper, (((1,), (0,)), ((), ())),
        precision=lax.Precision.HIGHEST, preferred_element_type=jnp.float32,
    )


def split_three(x):
    high = x.astype(jnp.bfloat16).astype(jnp.float32)
    rest = x - high
    mid = rest.astype(jnp.bfloat16).astype(jnp.float32)
    return high, mid, rest - mid


def final_states(length, p, k_ref, v_ref, rate, prior_ref, upper):
    heads, tokens = rate.shape
    live = lax.broadcasted_iota(jnp.int32, (heads, tokens), 1) < length
    terms = jnp.concatenate(split_three(jnp.where(live, rate, 0.0)), axis=0).astype(jnp.bfloat16)
    sums = jnp.dot(terms, upper, preferred_element_type=jnp.float32)
    total = sums[2 * heads:] + sums[heads:2 * heads] + sums[:heads]
    last = total[:, tokens - 1:tokens]
    keep = jnp.where(live, jnp.exp(last - total), 0.0)
    final = jnp.exp(last)
    states = []
    for h in range(heads):
        k = k_ref[p, :, head_of(h)].astype(jnp.float32).T
        decayed = (k * keep[h:h + 1, :]).astype(jnp.bfloat16)
        fresh = jnp.dot(decayed, v_ref[p, :, head_of(h)], preferred_element_type=jnp.float32)
        states.append(final[h:h + 1, :] * prior_ref[p, h] + fresh)
    return states


def fill_upper(upper_ref):
    row = lax.broadcasted_iota(jnp.int32, upper_ref.shape, 0)
    col = lax.broadcasted_iota(jnp.int32, upper_ref.shape, 1)
    upper_ref[...] = jnp.where(row <= col, 1.0, 0.0).astype(jnp.bfloat16)


def mixing_kernel(first, lengths_ref, owners_ref, k_ref, v_ref, ld_ref, prior_ref, out_ref, upper_ref):
    step = pl.program_id(0)
    each, heads = prior_ref.shape[:2]

    @pl.when(step == 0)
    def _():
        fill_upper(upper_ref)
        row = lax.broadcasted_iota(jnp.int32, out_ref.shape[2:], 0)
        named = jnp.zeros(out_ref.shape[2:], jnp.int32)
        for i in range(owners_ref.shape[0]):
            named = jnp.where(row == i, owners_ref[i], named)
        for j in range(out_ref.shape[0]):
            out_ref[j, out_ref.shape[1] - 1] = named.astype(jnp.float32)

    for p in range(each):
        r = step * each + p
        rate = ld_ref[p, first:first + heads]
        states = final_states(lengths_ref[r], p, k_ref, v_ref, rate, prior_ref, upper_ref[...])
        for h in range(heads):
            out_ref[:, r * heads + h] = states[h].reshape(HD // ROWS, ROWS, HD)


def owner_kernel(first, lengths_ref, owners_ref, k_ref, v_ref, ld_ref, prior_ref, out_ref, upper_ref):
    step = pl.program_id(0)
    each, heads = prior_ref.shape[:2]

    @pl.when(step == 0)
    def _():
        fill_upper(upper_ref)

    for p in range(each):
        r = step * each + p
        rate = ld_ref[p, first:first + heads]
        states = final_states(lengths_ref[r], p, k_ref, v_ref, rate, prior_ref, upper_ref[...])
        for h in range(heads):
            out_ref[owners_ref[r], h] = states[h]


def span_states(mixing, first, per, lengths, owned, keys, values, ld, prior, count):
    prompts, tokens, width = keys.shape
    heads = ld.shape[1]
    each = prompts // STEPS
    block = first // per
    if mixing:
        shape = (HD // ROWS, prompts * per + 1, ROWS, HD)
    else:
        shape = (count, per, HD, HD)
    return pl.pallas_call(
        functools.partial(mixing_kernel if mixing else owner_kernel, first),
        grid_spec=pltpu.PrefetchScalarGridSpec(
            num_scalar_prefetch=2,
            grid=(STEPS,),
            in_specs=[
                pl.BlockSpec((each, tokens, per * HD), lambda r, s, o: (r, 0, block)),
                pl.BlockSpec((each, tokens, per * HD), lambda r, s, o: (r, 0, block)),
                pl.BlockSpec((each, heads, tokens), lambda r, s, o: (r, 0, 0)),
                pl.BlockSpec((each, per, HD, HD), lambda r, s, o: (r, block, 0, 0)),
            ],
            out_specs=pl.BlockSpec(shape, lambda r, s, o: (0, 0, 0, 0)),
            scratch_shapes=[pltpu.VMEM((tokens, tokens), jnp.bfloat16)],
        ),
        out_shape=jax.ShapeDtypeStruct(shape, jnp.float32),
        compiler_params=pltpu.CompilerParams(vmem_limit_bytes=VMEM),
        cost_estimate=pl.CostEstimate(
            flops=2 * prompts * per * tokens * HD * HD,
            bytes_accessed=4 * prompts * tokens * per * HD + 8 * prompts * per * HD * HD,
            transcendentals=prompts * per * tokens,
        ),
        name="span_states",
    )(lengths, owned, keys, values, ld, prior)


def output_kernel(lengths_ref, q_ref, k_ref, v_ref, ld_ref, prior_ref, out_ref):
    r = pl.program_id(0)
    length = lengths_ref[r]
    heads, tokens = ld_ref.shape[1:]
    live_row = lax.broadcasted_iota(jnp.int32, (heads, tokens), 1) < length
    rate = jnp.where(live_row, ld_ref[0], 0.0)
    total_col = column_sums(rate)
    total_row = row_sums(rate)
    grow = jnp.exp(total_col)
    row = lax.broadcasted_iota(jnp.int32, (tokens, tokens), 0)
    col = lax.broadcasted_iota(jnp.int32, (tokens, tokens), 1)
    seen = (col <= row) & (col < length)
    live_col = lax.broadcasted_iota(jnp.int32, (tokens, HD), 0) < length
    for h in range(heads):
        q = q_ref[0, :, head_of(h)]
        score = lax.dot_general(
            q, k_ref[0, :, head_of(h)], (((1,), (1,)), ((), ())),
            preferred_element_type=jnp.float32,
        )
        gap = jnp.where(seen, total_col[:, h:h + 1] - total_row[h:h + 1, :], -jnp.inf)
        weight = (score * jnp.exp(gap)).astype(jnp.bfloat16)
        inner = jnp.dot(weight, v_ref[0, :, head_of(h)], preferred_element_type=jnp.float32)
        prior = prior_ref[0, h]
        high = prior.astype(jnp.bfloat16)
        rest = prior - high.astype(jnp.float32)
        mid = rest.astype(jnp.bfloat16)
        low = (rest - mid.astype(jnp.float32)).astype(jnp.bfloat16)
        carried = jnp.dot(q, low, preferred_element_type=jnp.float32)
        carried = carried + jnp.dot(q, mid, preferred_element_type=jnp.float32)
        carried = carried + jnp.dot(q, high, preferred_element_type=jnp.float32)
        out = inner + carried * grow[:, h:h + 1]
        out_ref[0, :, head_of(h)] = jnp.where(live_col, out, 0.0).astype(jnp.bfloat16)


def span_output(lengths, queries, keys, values, ld, prior):
    prompts, tokens, width = keys.shape
    heads = ld.shape[1]
    span = pl.BlockSpec((1, tokens, width), lambda r, s: (r, 0, 0))
    return pl.pallas_call(
        output_kernel,
        grid_spec=pltpu.PrefetchScalarGridSpec(
            num_scalar_prefetch=1,
            grid=(prompts,),
            in_specs=[
                span, span, span,
                pl.BlockSpec((1, heads, tokens), lambda r, s: (r, 0, 0)),
                pl.BlockSpec((1, heads, HD, HD), lambda r, s: (r, 0, 0, 0)),
            ],
            out_specs=span,
        ),
        out_shape=jax.ShapeDtypeStruct((prompts, tokens, width), jnp.bfloat16),
        compiler_params=pltpu.CompilerParams(vmem_limit_bytes=VMEM),
        cost_estimate=pl.CostEstimate(
            flops=2 * prompts * heads * tokens * HD * (2 * tokens + 3 * HD),
            bytes_accessed=8 * prompts * tokens * width + 4 * prompts * heads * HD * HD,
            transcendentals=prompts * heads * tokens * tokens,
        ),
        name="span_output",
    )(lengths, queries, keys, values, ld, prior)


def address_kernel(slots, n_pre, where_ref, *refs):
    held = refs[:slots]
    out_ref, groups_ref, present_ref, names, name_sems, sems = refs[slots:]
    per = out_ref.shape[3]
    rows = held[0].shape[1] - 1

    def fetch(j):
        return pltpu.make_async_copy(held[j].at[0, rows], names.at[j], name_sems.at[j])

    for j in range(slots):
        fetch(j).start()
    for j in range(slots):
        fetch(j).wait()
        groups_ref[j] = lax.rem(where_ref[0] + n_pre - ORDER[j], n_pre)
        present = jnp.int32(0)
        for r in range(rows // per):
            owner = names[j, r, 0].astype(jnp.int32)
            present = jnp.where(owner == where_ref[1], 1, present)
            pltpu.make_async_copy(
                held[j].at[:, pl.ds(r * per, per)], out_ref.at[owner, j], sems.at[j]
            ).start()
        present_ref[j] = present
    for j in range(slots):
        sent = held[j].at[:, pl.ds(0, rows)]
        pltpu.make_async_copy(sent, sent, sems.at[j]).wait()


def address(where, held, count, per):
    slots = len(held)
    halves = held[0].shape[0]
    smem = pl.BlockSpec(memory_space=pltpu.SMEM)
    return pl.pallas_call(
        functools.partial(address_kernel, slots, len(ORDER)),
        in_specs=[smem] + [pl.BlockSpec(memory_space=pltpu.VMEM) for _ in held],
        out_specs=[pl.BlockSpec(memory_space=pl.ANY), smem, smem],
        out_shape=[
            jax.ShapeDtypeStruct((count, slots, halves, per, ROWS, HD), jnp.float32),
            jax.ShapeDtypeStruct((slots,), jnp.int32),
            jax.ShapeDtypeStruct((slots,), jnp.int32),
        ],
        scratch_shapes=[
            pltpu.SMEM((slots, ROWS, HD), jnp.float32),
            pltpu.SemaphoreType.DMA((slots,)),
            pltpu.SemaphoreType.DMA((slots,)),
        ],
        compiler_params=pltpu.CompilerParams(vmem_limit_bytes=VMEM),
        name="address",
    )(where, *held)


def place_rows_kernel(groups_ref, present_ref, got_ref, out_ref, got, placed, in_sems, out_sems):
    pieces, slots, halves, per = got_ref.shape[:4]

    def fetch(j):
        return pltpu.make_async_copy(got_ref.at[:, j], got.at[j], in_sems.at[j])

    def store(j):
        return pltpu.make_async_copy(placed.at[j], out_ref.at[groups_ref[j], :, 0], out_sems.at[j])

    for j in range(slots):
        @pl.when(present_ref[j] > 0)
        def _():
            fetch(j).start()

    for j in range(slots):
        @pl.when(present_ref[j] == 0)
        def _():
            placed[j] = jnp.zeros(placed.shape[1:], jnp.float32)

        @pl.when(present_ref[j] > 0)
        def _():
            fetch(j).wait()
            for b in range(halves):
                for e in range(per):
                    placed[j, b, e] = got[j, :, b, e].reshape(pieces * ROWS, HD)

        store(j).start()
    for j in range(slots):
        store(j).wait()


def place_rows(groups, present, got, n_groups):
    pieces, slots, halves, per = got.shape[:4]
    smem = pl.BlockSpec(memory_space=pltpu.SMEM)
    hbm = pl.BlockSpec(memory_space=pl.ANY)
    return pl.pallas_call(
        place_rows_kernel,
        in_specs=[smem, smem, hbm],
        out_specs=hbm,
        out_shape=jax.ShapeDtypeStruct((n_groups, halves, PARTS, per, HD, HD), jnp.float32),
        scratch_shapes=[
            pltpu.VMEM((slots, pieces, halves, per, ROWS, HD), jnp.float32),
            pltpu.VMEM((slots, halves, per, HD, HD), jnp.float32),
            pltpu.SemaphoreType.DMA((slots,)),
            pltpu.SemaphoreType.DMA((slots,)),
        ],
        compiler_params=pltpu.CompilerParams(vmem_limit_bytes=VMEM),
        name="place_rows",
    )(groups, present, got)


def place_blocks_kernel(first, slots, groups_ref, present_ref, *refs):
    got = refs[:slots]
    out_ref, empty, sems = refs[slots + 1:]
    empty[...] = jnp.zeros(empty.shape, jnp.float32)
    for j in range(slots):
        target = out_ref.at[groups_ref[first + j], :, 1]

        @pl.when(present_ref[first + j] > 0)
        def _():
            pltpu.make_async_copy(got[j], target, sems.at[j]).start()

        @pl.when(present_ref[first + j] == 0)
        def _():
            pltpu.make_async_copy(empty, target, sems.at[j]).start()

    for j in range(slots):
        pltpu.make_async_copy(empty, empty, sems.at[j]).wait()


def place_blocks(first, groups, present, got, out):
    slots = len(got)
    smem = pl.BlockSpec(memory_space=pltpu.SMEM)
    hbm = pl.BlockSpec(memory_space=pl.ANY)
    return pl.pallas_call(
        functools.partial(place_blocks_kernel, first, slots),
        in_specs=[smem, smem] + [pl.BlockSpec(memory_space=pltpu.VMEM)] * slots + [hbm],
        out_specs=hbm,
        out_shape=jax.ShapeDtypeStruct(out.shape, jnp.float32),
        input_output_aliases={2 + slots: 0},
        scratch_shapes=[
            pltpu.VMEM(got[0].shape, jnp.float32),
            pltpu.SemaphoreType.DMA((slots,)),
        ],
        compiler_params=pltpu.CompilerParams(vmem_limit_bytes=VMEM),
        name="place_blocks",
    )(groups, present, *got, out)


def shifted(mixed, shift, n_pre):
    halves = mixed.shape[0] // n_pre
    goal = lax.rem(lax.axis_index("pre") + shift, n_pre)
    part = lax.dynamic_slice_in_dim(mixed, goal * halves, halves, 0)
    if shift == 0:
        return part
    return lax.ppermute(part, "pre", [(i, (i + shift) % n_pre) for i in range(n_pre)])


def over_dec(x):
    return lax.all_to_all(x, "dec", split_axis=0, concat_axis=0, tiled=True)


def shards(queries, keys, values, log_decay, prior_state, lengths, owners):
    n_pre = lax.axis_size("pre")
    n_dec = lax.axis_size("dec")
    heads = prior_state.shape[1]
    ld = jnp.swapaxes(log_decay, 1, 2)
    spans = (lengths, owners[:, 0], keys, values, ld, prior_state, n_dec)
    per = heads // PARTS
    where = jnp.stack([lax.axis_index("pre"), lax.axis_index("dec")]).astype(jnp.int32)
    mixed = over_dec(span_states(True, 0, per, *spans))
    named = span_states(False, per, per, *spans)
    named, mixed, where = lax.optimization_barrier((named, mixed, where))
    owned = over_dec(named)
    held = [shifted(mixed, m, n_pre) for m in ORDER]
    blocks = [shifted(owned, m, n_pre) for m in ORDER]
    held, blocks[:FIRST] = lax.optimization_barrier((held, blocks[:FIRST]))
    sent, groups, present = address(where, held, n_dec, per)
    got = over_dec(sent)
    got, queries = lax.optimization_barrier((got, queries))
    prefill_out = span_output(lengths, queries, keys, values, ld, prior_state)
    decode_state = place_rows(groups, present, got, n_pre)
    decode_state = place_blocks(0, groups, present, blocks[:LATE], decode_state)
    decode_state = place_blocks(LATE, groups, present, blocks[LATE:], decode_state)
    return prefill_out, decode_state.reshape(n_pre, -1, HD, HD)


def solution(mesh):
    placed = (
        P(("rep", "pre"), None, "dec"),
        P(("rep", "pre"), None, "dec"),
        P(("rep", "pre"), None, "dec"),
        P(("rep", "pre"), None, "dec"),
        P(("rep", "pre"), "dec", None, None),
        P(("rep", "pre")),
        P(("rep", "pre"), None),
    )
    return jax.shard_map(
        shards,
        mesh=mesh,
        in_specs=placed,
        out_specs=(P(("rep", "pre"), None, "dec"), P(("rep", "dec"), "pre", None, None)),
        check_vma=False,
    )
```
